32 devices in a mesh: lon: 8 (over y, x, core), lat: 4 (over z).
Axes of the slice: x: 2, y: 2, z: 4, core: 2. Of those that a mesh axis runs over, the one named last changes fastest.
Arguments:
- state: float32 [2, 4, 360, 512], P(None, None, 'lon', 'lat'), may hold values from -6 to 6
- courant: float32 [2, 360, 512], P(None, 'lon', 'lat'), may hold values from 1 to 2160
- band_mask: int32 [512], P('lat'), may hold values 0 or 1
Outputs:
- updated: float32 [2, 4, 360, 512], P(None, None, 'lon', 'lat')
The draws below stay inside these ranges and needn't reach their ends.
All inputs are finite; a program needn't handle non-finite values. No bound on the sum of `band_mask` on one device may be relied on, other than what follows from the above.
Results may differ from the reference program's by a relative error of at most 0.00029.
Values sent between devices are 32-bit elements; how exact they have to be, the bound alone decides.
A program may use at most 64 MiB of HBM per device.

```python
import jax
import jax.numpy as jnp
from jax import lax

VERTICAL_LAYERS = 2
ITERS = 2
MERIDIAN_POINTS = 360
PARALLEL_CIRCLES = 512


def draw_courant(key, part):
    stochastic_seeds = jax.random.split(key, 5)
    slow_share = 0.5
    slow = jax.random.uniform(stochastic_seeds[0], (VERTICAL_LAYERS, 1, PARALLEL_CIRCLES), jnp.float32) < slow_share
    spot = jax.random.uniform(stochastic_seeds[1], (VERTICAL_LAYERS, 1, PARALLEL_CIRCLES), jnp.float32)
    fast_lo = jnp.log(30.0)
    fast_hi = jnp.log(MERIDIAN_POINTS / 2.0)
    slow_lo = jnp.log(MERIDIAN_POINTS / 2.0)
    slow_hi = jnp.log(3.0 * MERIDIAN_POINTS)
    parallel_speed = jnp.where(slow, jnp.exp(slow_lo + spot * (slow_hi - slow_lo)), jnp.exp(fast_lo + spot * (fast_hi - fast_lo)))
    decay_multiplier = jnp.exp(jax.random.uniform(stochastic_seeds[2], (VERTICAL_LAYERS, MERIDIAN_POINTS, PARALLEL_CIRCLES), jnp.float32, jnp.log(0.5), jnp.log(2.0)))
    repeated_passes = jax.random.uniform(stochastic_seeds[3], (VERTICAL_LAYERS, MERIDIAN_POINTS, PARALLEL_CIRCLES), jnp.float32) < 3.0 / MERIDIAN_POINTS
    tiny_offset = jax.random.uniform(stochastic_seeds[4], (VERTICAL_LAYERS, MERIDIAN_POINTS, PARALLEL_CIRCLES), jnp.float32, 1.0, 4.0)
    return jnp.where(repeated_passes, tiny_offset, parallel_speed * decay_multiplier).astype(jnp.float32)


def touch_ends(drawn, rng, smallest, high):
    longest = drawn.shape.index(max(drawn.shape))
    spots = []
    for shift in (0, 1):
        where = [jax.random.randint(jax.random.fold_in(rng, axis), (), 0, length) for axis, length in enumerate(drawn.shape)]
        where[longest] = (where[longest] + shift) % drawn.shape[longest]
        spots.append(tuple(where))
    return drawn.at[spots[0]].set(smallest).at[spots[1]].set(high)


def block_levels(key, dims, shards, least, top_value):
    def one(axis_at, shards_of):
        steps = jax.random.uniform(jax.random.fold_in(jax.random.fold_in(key, 6), axis_at), (shards_of,), jnp.float32, least / len(shards), top_value / len(shards))
        return jnp.repeat(jnp.exp(steps), dims[axis_at] // shards_of).reshape((-1,) + (1,) * (len(dims) - axis_at - 1))

    factor_of = one(*shards[0])
    for cut in shards[1:]:
        factor_of = factor_of * one(*cut)
    return factor_of


def noise(own_key, dims, spread, most, cuts=(), kind=jnp.bfloat16):
    gain = block_levels(own_key, dims, cuts, -0.22, 0.18) if cuts else 1.0
    values = jax.random.normal(own_key, dims, jnp.float32) * spread * gain
    return jnp.minimum(jnp.maximum(values, -most), most).astype(kind)


def setup_inputs(seed: int = 0) -> dict:
    seeds = jax.random.split(jax.random.key(seed), 4)
    state = noise(seeds[0], (VERTICAL_LAYERS, 4, MERIDIAN_POINTS, PARALLEL_CIRCLES), 1.0, 6.0, ((2, 8), (3, 4)), jnp.float32)
    courant = draw_courant(jax.random.fold_in(seeds[3], 71), 0)
    band_mask = touch_ends((jax.random.randint(seeds[2], (PARALLEL_CIRCLES,), 0, 4) < 3).astype(jnp.int32), jax.random.fold_in(seeds[2], 1), 0, 1)
    return dict(state=state, courant=courant, band_mask=band_mask)


def tendency(field, turning):
    half_cycle = field.shape[2] // 2
    flips = jnp.array([-1.0, -1.0, 1.0, 1.0], jnp.float32)[None, :, None]
    north_rim = jnp.roll(field[..., 0], half_cycle, axis=2) * flips
    south_rim = jnp.roll(field[..., -1], half_cycle, axis=2) * flips
    north_rows = jnp.concatenate([north_rim[..., None], field[..., :-1]], axis=3)
    south_rows = jnp.concatenate([field[..., 1:], south_rim[..., None]], axis=3)
    east_cells = jnp.roll(field, -1, axis=2)
    west_cells = jnp.roll(field, 1, axis=2)
    u_wind = field[:, 0:1]
    v_wind = field[:, 1:2]
    result = 0.1 * (east_cells + west_cells - 2.0 * field) + 0.1 * (north_rows + south_rows - 2.0 * field)
    result = result - 0.25 * v_wind * (north_rows - south_rows)
    coriolis = jnp.concatenate([turning * v_wind, -turning * u_wind, jnp.zeros_like(field[:, 2:])], axis=1)
    return result + coriolis


def zonal_solve(star, courant):
    inverse = 1.0 / (1.0 + courant)
    decay_multiplier = courant * inverse
    items = (jnp.moveaxis(star, 2, 0), jnp.moveaxis(decay_multiplier, 1, 0), jnp.moveaxis(inverse, 1, 0))

    def advance(carry, item):
        value, product = carry
        source, rate, weight = item
        value = rate[:, None, :] * value + source * weight[:, None, :]
        product = rate * product
        return (value, product), (value, product)

    start_value = jnp.zeros((star.shape[0], star.shape[1], star.shape[3]), jnp.float32)
    start_product = jnp.ones((star.shape[0], star.shape[3]), jnp.float32)
    (last_value, last_product), (values, products) = lax.scan(advance, (start_value, start_product), items)
    wrapped = last_value / (1.0 - last_product)[:, None, :]
    solved = values + products[:, :, None, :] * wrapped[None]
    return jnp.moveaxis(solved, 0, 2)


def reference(state, courant, band_mask):
    total_rows = state.shape[3]
    row_ids = jnp.arange(total_rows, dtype=jnp.int32)
    latitude = jnp.pi / 2 - (row_ids.astype(jnp.float32) + 0.5) * jnp.pi / total_rows
    turning = 0.5 * jnp.sin(latitude)
    in_band = (band_mask == 1)[None, None, None, :]
    estimate = state
    for sweep in range(ITERS):
        middle = 0.5 * (state + estimate)
        star = state + tendency(middle, turning)
        solved = zonal_solve(star, courant)
        estimate = jnp.where(in_band, solved, star)
    return estimate
```

```python
import functools

import jax
import jax.numpy as jnp
from jax import lax
from jax.experimental import pallas as pl
from jax.experimental.pallas import tpu as pltpu
from jax.sharding import PartitionSpec as P

ITERS = 2
MESH = pl.DeviceIdType.MESH


def kernel(n, m, x_ref, c_ref, mask_ref, out_ref, X, inv8, carried, part, mid,
           lonh, lats, lath, gains, ends, own,
           lon_send, lon_recv, lat_send, lat_recv, all_send, all_recv):
    levels, comps, L, R = x_ref.shape
    S = levels * comps
    lon = lax.axis_index("lon")
    lat = lax.axis_index("lat")
    east = lax.rem(lon + 1, n)
    west = lax.rem(lon + n - 1, n)
    across = lax.rem(lon + n // 2, n)
    first = lat == 0
    last = lat == m - 1
    north = (jnp.where(first, across, lon), jnp.where(first, lat, lat - 1))
    south = (jnp.where(last, across, lon), jnp.where(last, lat, lat + 1))
    north_slot = jnp.where(first, 0, 1)
    south_slot = jnp.where(last, 1, 0)

    barrier = pltpu.get_barrier_semaphore()

    def greet(k, _):
        pl.semaphore_signal(barrier, inc=1, device_id=(lax.rem(lon + k, n), lat), device_id_type=MESH)
        return 0

    lax.fori_loop(1, n, greet, 0)
    pl.semaphore_signal(barrier, inc=1, device_id=north, device_id_type=MESH)
    pl.semaphore_signal(barrier, inc=1, device_id=south, device_id_type=MESH)

    for g in range(0, L, 8):
        w = min(8, L - g)
        block = x_ref[:, :, g:g + w, :].reshape(S, w, R)
        X[g:g + w] = jnp.swapaxes(block, 0, 1)

    sub = lax.broadcasted_iota(jnp.int32, (S, R), 0)
    lane = lax.broadcasted_iota(jnp.int32, (S, R), 1)
    comp = sub % comps
    lower = sub < comps

    def by_level(rows):
        return jnp.where(lower, jnp.broadcast_to(rows[0], (S, R)), jnp.broadcast_to(rows[1], (S, R)))

    row_ids = (lat * R + lane).astype(jnp.float32)
    turning = 0.5 * jnp.sin(jnp.pi / 2 - (row_ids + 0.5) * (jnp.pi / (R * m)))
    turn_u = jnp.where(comp == 0, turning, 0.0)
    turn_v = jnp.where(comp == 1, -turning, 0.0)
    flips = jnp.where(comp < 2, -1.0, 1.0)
    flip_n = jnp.where(first, flips, 1.0)
    flip_s = jnp.where(last, flips, 1.0)

    def pack(src, it):
        rim_n = jnp.zeros((S, R), jnp.float32)
        rim_s = jnp.zeros((S, R), jnp.float32)
        for i in range(L):
            value = src[i]
            rim_n = jnp.where(lane == i, value if i == 0 else pltpu.roll(value, i, 1), rim_n)
            rim_s = jnp.where(lane == i, pltpu.roll(value, i + 1, 1), rim_s)
        lats[it, 0] = rim_n
        lats[it, 1] = rim_s

    def halo_copies(src, it):
        return [
            pltpu.make_async_remote_copy(
                src_ref=src.at[L - 1], dst_ref=lonh.at[it, 0], send_sem=lon_send.at[it, 0],
                recv_sem=lon_recv.at[it, 0], device_id=(east, lat), device_id_type=MESH),
            pltpu.make_async_remote_copy(
                src_ref=src.at[0], dst_ref=lonh.at[it, 1], send_sem=lon_send.at[it, 1],
                recv_sem=lon_recv.at[it, 1], device_id=(west, lat), device_id_type=MESH),
            pltpu.make_async_remote_copy(
                src_ref=lats.at[it, 0], dst_ref=lath.at[it, north_slot], send_sem=lat_send.at[it, 0],
                recv_sem=lat_recv.at[it, north_slot], device_id=north, device_id_type=MESH),
            pltpu.make_async_remote_copy(
                src_ref=lats.at[it, 1], dst_ref=lath.at[it, south_slot], send_sem=lat_send.at[it, 1],
                recv_sem=lat_recv.at[it, south_slot], device_id=south, device_id_type=MESH),
        ]

    def gather_start(src, dst, k_sem):
        def send(k, _):
            pltpu.make_async_remote_copy(
                src_ref=src, dst_ref=dst.at[k - 1], send_sem=all_send.at[k_sem],
                recv_sem=all_recv.at[k_sem], device_id=(lax.rem(lon + n - k, n), lat),
                device_id_type=MESH).start()
            return 0
        lax.fori_loop(1, n, send, 0)

    def gather_wait(dst, sem):
        pltpu.make_async_copy(dst, dst, sem).wait()

    pack(X, 0)
    pl.semaphore_wait(barrier, n + 1)
    halos = halo_copies(X, 0)
    for copy in halos:
        copy.start()

    band = mask_ref[...] == 1
    for i in range(L):
        rows = [jnp.where(band, 1.0 / (1.0 + c_ref[l, i:i + 1, :]), 1.0) for l in range(levels)]
        inv8[i] = by_level(rows)
    gain = 1.0 - inv8[0]
    carried[0] = gain
    for i in range(1, L):
        gain = gain * (1.0 - inv8[i])
        carried[i] = gain
    gather_start(carried.at[L - 1], gains, 0)

    ring = None
    for it in range(ITERS):
        src = X if it == 0 else mid
        for index in (0, 1):
            halos[index].wait_recv()
        for index in (0, 1):
            pltpu.make_async_copy(lath.at[it, index], lath.at[it, index], lat_recv.at[it, index]).wait()
        rim_n = lath[it, 0] * flip_n
        rim_s = lath[it, 1] * flip_s
        rim_w = lonh[it, 0]
        rim_e = lonh[it, 1]
        value = jnp.zeros((S, R), jnp.float32)
        for i in range(L):
            x = src[i]
            e = src[i + 1] if i + 1 < L else rim_e
            w = src[i - 1] if i > 0 else rim_w
            no = jnp.where(lane == 0, rim_n if i == 0 else pltpu.roll(rim_n, R - i, 1), pltpu.roll(x, 1, 1))
            so = jnp.where(lane == R - 1, pltpu.roll(rim_s, R - 1 - i, 1), pltpu.roll(x, R - 1, 1))
            u = by_level([src[i, l * comps:l * comps + 1, :] for l in range(levels)])
            v = by_level([src[i, l * comps + 1:l * comps + 2, :] for l in range(levels)])
            star = X[i] + (0.1 * (e + w + no + so) - 0.4 * x) - (0.25 * v) * (no - so) + (turn_u * v + turn_v * u)
            inv = inv8[i]
            value = (1.0 - inv) * value + star * inv
            part[i] = value
        own[it] = value
        gather_start(own.at[it], ends.at[it], 1 + it)
        if it == 0:
            gather_wait(gains, all_recv.at[0])
            total = carried[L - 1]
            if n <= 16:
                for k in range(n - 1):
                    total = total * gains[k]
            else:
                total = lax.fori_loop(0, n - 1, lambda k, t: t * gains[k], total)
            ring = 1.0 / (1.0 - total)
        gather_wait(ends.at[it], all_recv.at[1 + it])
        run = own[it]
        if n <= 16:
            for k in range(n - 1):
                run = run * gains[k] + ends[it, k]
        else:
            run = lax.fori_loop(0, n - 1, lambda k, r: r * gains[k] + ends[it, k], run)
        inflow = run * ring
        if it + 1 < ITERS:
            for i in range(L):
                mid[i] = 0.5 * (X[i] + (part[i] + carried[i] * inflow))
            pack(mid, it + 1)
            for copy in halos:
                copy.wait_send()
            halos = halo_copies(mid, it + 1)
            for copy in halos:
                copy.start()
        else:
            for i in range(L):
                out_ref[i] = part[i] + carried[i] * inflow
    for copy in halos:
        copy.wait_send()
    for k in range(3):
        gather_wait(gains, all_send.at[k])


def local(n, m, state, courant, band_mask):
    levels, comps, L, R = state.shape
    S = levels * comps
    f32 = jnp.float32
    cell = (L, S, R)
    out = pl.pallas_call(
        functools.partial(kernel, n, m),
        out_shape=jax.ShapeDtypeStruct(cell, f32),
        in_specs=[pl.BlockSpec(memory_space=pltpu.VMEM)] * 3,
        out_specs=pl.BlockSpec(memory_space=pltpu.VMEM),
        scratch_shapes=[
            pltpu.VMEM(cell, f32),
            pltpu.VMEM(cell, f32),
            pltpu.VMEM(cell, f32),
            pltpu.VMEM(cell, f32),
            pltpu.VMEM(cell, f32),
            pltpu.VMEM((ITERS, 2, S, R), f32),
            pltpu.VMEM((ITERS, 2, S, R), f32),
            pltpu.VMEM((ITERS, 2, S, R), f32),
            pltpu.VMEM((n - 1, S, R), f32),
            pltpu.VMEM((ITERS, n - 1, S, R), f32),
            pltpu.VMEM((ITERS, S, R), f32),
            pltpu.SemaphoreType.DMA((ITERS, 2)),
            pltpu.SemaphoreType.DMA((ITERS, 2)),
            pltpu.SemaphoreType.DMA((ITERS, 2)),
            pltpu.SemaphoreType.DMA((ITERS, 2)),
            pltpu.SemaphoreType.DMA((3,)),
            pltpu.SemaphoreType.DMA((3,)),
        ],
        compiler_params=pltpu.CompilerParams(
            collective_id=0, has_side_effects=True, vmem_limit_bytes=16 * 2**20),
    )(state, courant, band_mask.reshape(1, R))
    return out.transpose(1, 0, 2).reshape(state.shape)


def solution(mesh):
    n, m = mesh.shape["lon"], mesh.shape["lat"]
    in_specs = (P(None, None, "lon", "lat"), P(None, "lon", "lat"), P("lat"))
    out_specs = P(None, None, "lon", "lat")
    return jax.shard_map(functools.partial(local, n, m), mesh=mesh, in_specs=in_specs, out_specs=out_specs, check_vma=False)
```

```python
import functools

import jax
import jax.numpy as jnp
from jax import lax
from jax.experimental import pallas as pl
from jax.experimental.pallas import tpu as pltpu
from jax.sharding import PartitionSpec as P

ITERS = 2
MESH = pl.DeviceIdType.MESH


def kernel(n, m, x_hbm, c_hbm, mask_hbm, out_ref, x_in, c_in, mask_ref, X, inv8, carried, part, fed, edge, mid,
           lonh, lats, lath, gains, ends, own,
           in_sem, lon_send, lon_recv, lat_send, lat_recv, all_send, all_recv):
    levels, L, comps, R = x_in.shape
    S = levels * comps
    lon = lax.axis_index("lon")
    lat = lax.axis_index("lat")
    east = lax.rem(lon + 1, n)
    west = lax.rem(lon + n - 1, n)
    across = lax.rem(lon + n // 2, n)
    first = lat == 0
    last = lat == m - 1
    north = (jnp.where(first, across, lon), jnp.where(first, lat, lat - 1))
    south = (jnp.where(last, across, lon), jnp.where(last, lat, lat + 1))
    north_slot = jnp.where(first, 0, 1)
    south_slot = jnp.where(last, 1, 0)

    def over_ring(step):
        if n <= 16:
            for k in range(1, n):
                step(k)
        else:
            lax.fori_loop(1, n, lambda k, _: (step(k), 0)[1], 0)

    barrier = pltpu.get_barrier_semaphore()
    x_copy = pltpu.make_async_copy(x_hbm, x_in, in_sem.at[0])
    c_copy = pltpu.make_async_copy(c_hbm, c_in, in_sem.at[1])
    mask_copy = pltpu.make_async_copy(mask_hbm, mask_ref, in_sem.at[2])
    x_copy.start()
    c_copy.start()
    mask_copy.start()
    pl.semaphore_signal(barrier, inc=1, device_id=north, device_id_type=MESH)
    pl.semaphore_signal(barrier, inc=1, device_id=south, device_id_type=MESH)
    over_ring(lambda k: pl.semaphore_signal(
        barrier, inc=1, device_id=(lax.rem(lon + k, n), lat), device_id_type=MESH))

    sub = lax.broadcasted_iota(jnp.int32, (S, R), 0)
    lane = lax.broadcasted_iota(jnp.int32, (S, R), 1)
    comp = sub % comps
    lower = sub < comps
    is_north = lane == 0
    is_south = lane == R - 1
    even = lane % 2 == 0
    pair = ((lane + 1) % R) // 2

    def by_level(rows):
        return jnp.where(lower, jnp.broadcast_to(rows[0], (S, R)), jnp.broadcast_to(rows[1], (S, R)))

    row_ids = (lat * R + lane).astype(jnp.float32)
    turning = 0.5 * jnp.sin(jnp.pi / 2 - (row_ids + 0.5) * (jnp.pi / (R * m)))
    turn_u = jnp.where(comp == 0, turning, 0.0)
    turn_v = jnp.where(comp == 1, -turning, 0.0)
    flips = jnp.where(comp < 2, -1.0, 1.0)

    def pack(values, it):
        rim = values(0)
        for i in range(1, L):
            rim = jnp.where(pair == i, pltpu.roll(values(i), 2 * i, 1), rim)
        lats[it] = rim

    def halo_copies(src, it):
        return [
            pltpu.make_async_remote_copy(
                src_ref=lats.at[it], dst_ref=lath.at[it, north_slot], send_sem=lat_send.at[it, 0],
                recv_sem=lat_recv.at[it, north_slot], device_id=north, device_id_type=MESH),
            pltpu.make_async_remote_copy(
                src_ref=lats.at[it], dst_ref=lath.at[it, south_slot], send_sem=lat_send.at[it, 1],
                recv_sem=lat_recv.at[it, south_slot], device_id=south, device_id_type=MESH),
            pltpu.make_async_remote_copy(
                src_ref=src.at[L - 1], dst_ref=lonh.at[it, 0], send_sem=lon_send.at[it, 0],
                recv_sem=lon_recv.at[it, 0], device_id=(east, lat), device_id_type=MESH),
            pltpu.make_async_remote_copy(
                src_ref=src.at[0], dst_ref=lonh.at[it, 1], send_sem=lon_send.at[it, 1],
                recv_sem=lon_recv.at[it, 1], device_id=(west, lat), device_id_type=MESH),
        ]

    def gather_start(src, dst, sem):
        over_ring(lambda k: pltpu.make_async_remote_copy(
            src_ref=src, dst_ref=dst.at[k - 1], send_sem=all_send.at[sem],
            recv_sem=all_recv.at[sem], device_id=(lax.rem(lon + n - k, n), lat),
            device_id_type=MESH).start())

    def wait_for(ref, sem):
        pltpu.make_async_copy(ref, ref, sem).wait()

    def fold(step, start):
        if n <= 16:
            for k in range(n - 1):
                start = step(k, start)
            return start
        return lax.fori_loop(0, n - 1, step, start)

    x_copy.wait()
    for i in range(L):
        X[i] = jnp.concatenate([x_in[l, i] for l in range(levels)], axis=0)
    pack(lambda i: X[i], 0)
    pl.semaphore_wait(barrier, n + 1)
    halos = halo_copies(X, 0)
    for copy in halos:
        copy.start()

    c_copy.wait()
    mask_copy.wait()
    band = mask_ref[...] == 1
    for i in range(L):
        inv = jnp.where(band, 1.0 / (1.0 + c_in[i]), 1.0)
        inv8[i] = by_level([inv[l:l + 1] for l in range(levels)])
    gain = 1.0 - inv8[0]
    carried[0] = gain
    for i in range(1, L):
        gain = gain * (1.0 - inv8[i])
        carried[i] = gain
    gather_start(carried.at[L - 1], gains, 0)

    ring = None
    for it in range(ITERS):
        src = X if it == 0 else mid
        for i in range(L):
            x = src[i]
            no = jnp.where(is_north, 0.0, pltpu.roll(x, 1, 1))
            so = jnp.where(is_south, 0.0, pltpu.roll(x, R - 1, 1))
            u = by_level([src[i, l * comps:l * comps + 1, :] for l in range(levels)])
            v = by_level([src[i, l * comps + 1:l * comps + 2, :] for l in range(levels)])
            if i == 0:
                sides = src[1]
            elif i == L - 1:
                sides = src[L - 2]
            else:
                sides = src[i + 1] + src[i - 1]
            quarter = 0.25 * v
            star = X[i] + (0.1 * (sides + no + so) - 0.4 * x) - quarter * (no - so) + (turn_u * v + turn_v * u)
            inv = inv8[i]
            fed[i] = star * inv
            edge[i] = inv * jnp.where(is_north, 0.1 - quarter, jnp.where(is_south, 0.1 + quarter, 0.0))
        wait_for(lath.at[it, 0], lat_recv.at[it, 0])
        wait_for(lath.at[it, 1], lat_recv.at[it, 1])
        rim_n = lath[it, 0]
        rim_n = jnp.where(first, rim_n * flips, pltpu.roll(rim_n, 1, 1))
        rim_s = lath[it, 1]
        rim_s = jnp.where(last, rim_s * flips, pltpu.roll(rim_s, R - 1, 1))
        rim = jnp.where(even, rim_n, rim_s)
        halos[2].wait_recv()
        halos[3].wait_recv()
        value = None
        for i in range(L):
            inv = inv8[i]
            feed = fed[i] + edge[i] * (pltpu.roll(rim, (R - 2 * i) % R, 1) if i else rim)
            if i == 0:
                feed = feed + (0.1 * inv) * lonh[it, 0]
            if i == L - 1:
                feed = feed + (0.1 * inv) * lonh[it, 1]
            value = feed if i == 0 else (1.0 - inv) * value + feed
            part[i] = value
        own[it] = value
        gather_start(own.at[it], ends.at[it], 1 + it)
        if it == 0:
            wait_for(gains, all_recv.at[0])
            ring = 1.0 / (1.0 - fold(lambda k, t: t * gains[k], carried[L - 1]))
        wait_for(ends.at[it], all_recv.at[1 + it])
        inflow = fold(lambda k, r: r * gains[k] + ends[it, k], value) * ring
        if it + 1 < ITERS:
            for i in range(L):
                mid[i] = 0.5 * (X[i] + (part[i] + carried[i] * inflow))
            pack(lambda i: mid[i], it + 1)
            for copy in halos:
                copy.wait_send()
            halos = halo_copies(mid, it + 1)
            for copy in halos:
                copy.start()
        else:
            for i in range(L):
                result = part[i] + carried[i] * inflow
                for l in range(levels):
                    out_ref[l, i] = result[l * comps:(l + 1) * comps]
    for copy in halos:
        copy.wait_send()
    for sem in range(1 + ITERS):
        wait_for(gains, all_send.at[sem])


def local(n, m, state, courant, band_mask):
    levels, comps, L, R = state.shape
    S = levels * comps
    f32 = jnp.float32
    cell = pltpu.VMEM((L, S, R), f32)
    out = pl.pallas_call(
        functools.partial(kernel, n, m),
        out_shape=jax.ShapeDtypeStruct((levels, L, comps, R), f32),
        in_specs=[
            pl.BlockSpec(memory_space=pltpu.HBM),
            pl.BlockSpec(memory_space=pltpu.HBM),
            pl.BlockSpec(memory_space=pltpu.HBM),
        ],
        out_specs=pl.BlockSpec(memory_space=pltpu.VMEM),
        scratch_shapes=[
            pltpu.VMEM((levels, L, comps, R), f32),
            pltpu.VMEM((L, levels, R), f32),
            pltpu.VMEM((1, R), jnp.int32),
            cell, cell, cell, cell, cell, cell, cell,
            pltpu.VMEM((ITERS, 2, S, R), f32),
            pltpu.VMEM((ITERS, S, R), f32),
            pltpu.VMEM((ITERS, 2, S, R), f32),
            pltpu.VMEM((n - 1, S, R), f32),
            pltpu.VMEM((ITERS, n - 1, S, R), f32),
            pltpu.VMEM((ITERS, S, R), f32),
            pltpu.SemaphoreType.DMA((3,)),
            pltpu.SemaphoreType.DMA((ITERS, 2)),
            pltpu.SemaphoreType.DMA((ITERS, 2)),
            pltpu.SemaphoreType.DMA((ITERS, 2)),
            pltpu.SemaphoreType.DMA((ITERS, 2)),
            pltpu.SemaphoreType.DMA((1 + ITERS,)),
            pltpu.SemaphoreType.DMA((1 + ITERS,)),
        ],
        compiler_params=pltpu.CompilerParams(
            collective_id=0, has_side_effects=True, vmem_limit_bytes=64 * 2**20 - 2**17),
    )(state.transpose(0, 2, 1, 3), courant.transpose(1, 0, 2), band_mask.reshape(1, R))
    return out.transpose(0, 2, 1, 3)


def solution(mesh):
    n, m = mesh.shape["lon"], mesh.shape["lat"]
    in_specs = (P(None, None, "lon", "lat"), P(None, "lon", "lat"), P("lat"))
    out_specs = P(None, None, "lon", "lat")
    return jax.shard_map(functools.partial(local, n, m), mesh=mesh, in_specs=in_specs, out_specs=out_specs, check_vma=False)
```

```python
import functools

import jax
import jax.numpy as jnp
from jax import lax
from jax.experimental import pallas as pl
from jax.experimental.pallas import tpu as pltpu
from jax.sharding import PartitionSpec as P

MESH = pl.DeviceIdType.MESH


def kernel(n, m, x_hbm, c_hbm, mask_hbm, out_ref, x_in, c_in, mask_ref, X, inv8, carried, part, fed, edge, mid,
           side_inv, side_x, side_part, side_carried, rows,
           rim_out, rim_in, ring_out, ring_in, ends_out, ends_in, last_out, last_in,
           in_sem, send_sem, recv_sem):
    levels, L, comps, R = x_in.shape
    S = levels * comps
    lon = lax.axis_index("lon")
    lat = lax.axis_index("lat")
    first = lat == 0
    last = lat == m - 1
    north_lat = jnp.where(first, lat, lat - 1)
    south_lat = jnp.where(last, lat, lat + 1)
    north_shift = jnp.where(first, n // 2, 0)
    south_shift = jnp.where(last, n // 2, 0)
    north_slot = jnp.where(first, 0, 1)
    south_slot = jnp.where(last, 1, 0)

    def shifted(k):
        return lax.rem(lon + (k + n), n)

    rim_peers = [
        (shifted(shift + e), to_lat, slot, e)
        for e in (0, 1, -1)
        for shift, to_lat, slot in ((north_shift, north_lat, north_slot), (south_shift, south_lat, south_slot))
    ]

    def over_middle(step, low, high):
        if n <= 16:
            for k in range(low, high):
                step(k)
        else:
            lax.fori_loop(low, high, lambda k, _: (step(k), 0)[1], 0)

    barrier = pltpu.get_barrier_semaphore()
    x_copy = pltpu.make_async_copy(x_hbm, x_in, in_sem.at[0])
    c_copy = pltpu.make_async_copy(c_hbm, c_in, in_sem.at[1])
    mask_copy = pltpu.make_async_copy(mask_hbm, mask_ref, in_sem.at[2])
    x_copy.start()
    c_copy.start()
    mask_copy.start()
    for to_lon, to_lat, _, _ in rim_peers:
        pl.semaphore_signal(barrier, inc=1, device_id=(to_lon, to_lat), device_id_type=MESH)
    over_middle(lambda k: pl.semaphore_signal(
        barrier, inc=1, device_id=(shifted(k), lat), device_id_type=MESH), 1, n)

    sub = lax.broadcasted_iota(jnp.int32, (S, R), 0)
    lane = lax.broadcasted_iota(jnp.int32, (S, R), 1)
    comp = sub % comps
    lower = sub < comps
    is_north = lane == 0
    is_south = lane == R - 1
    even = lane % 2 == 0
    pair = ((lane + 1) % R) // 2
    second_pair = jnp.where(even, ((lane + 2) % R) // 2, lane // 2)

    def roll(value, shift):
        shift = shift % R
        return pltpu.roll(value, shift, 1) if shift else value

    def by_level(values):
        return jnp.where(lower, jnp.broadcast_to(values[0], (S, R)), jnp.broadcast_to(values[1], (S, R)))

    def winds(ref, i):
        u = by_level([ref[i, l * comps:l * comps + 1, :] for l in range(levels)])
        v = by_level([ref[i, l * comps + 1:l * comps + 2, :] for l in range(levels)])
        return u, v

    def turns(row_ids):
        turning = 0.5 * jnp.sin(jnp.pi / 2 - (row_ids.astype(jnp.float32) + 0.5) * (jnp.pi / (R * m)))
        return jnp.where(comp == 0, turning, 0.0), jnp.where(comp == 1, -turning, 0.0)

    turn_u, turn_v = turns(lat * R + lane)
    side_turn_u, side_turn_v = turns(jnp.where(
        even, jnp.where(first, 0, lat * R - 1), jnp.where(last, R * m - 1, lat * R + R)))
    flips = jnp.where(comp < 2, -1.0, 1.0)

    def remote(src, dst, sem, device):
        return pltpu.make_async_remote_copy(
            src_ref=src, dst_ref=dst, send_sem=send_sem.at[sem], recv_sem=recv_sem.at[sem],
            device_id=device, device_id_type=MESH)

    def wait_for(ref, sem):
        pltpu.make_async_copy(ref, ref, sem).wait()

    def fold(step, start, low, high):
        if n <= 16:
            for k in range(low, high):
                start = step(k, start)
            return start
        return lax.fori_loop(low, high, step, start)

    x_copy.wait()
    for i in range(L):
        value = jnp.concatenate([x_in[l, i] for l in range(levels)], axis=0)
        X[i] = value
        moved = roll(value, 2 * i)
        rim0 = moved if i == 0 else jnp.where(pair == i, moved, rim0)
        rim1 = moved if i == 0 else jnp.where(second_pair == i, moved, rim1)
    rim_out[0] = rim0
    rim_out[2] = rim1
    c_copy.wait()
    mask_copy.wait()
    band = mask_ref[...] == 1
    for i in range(L):
        inv = jnp.where(band, 1.0 / (1.0 + c_in[i]), 1.0)
        inv = by_level([inv[l:l + 1] for l in range(levels)])
        inv8[i] = inv
        moved = roll(inv, 2 * i)
        rim2 = moved if i == 0 else jnp.where(pair == i, moved, rim2)
    rim_out[1] = rim2

    pl.semaphore_wait(barrier, n - 1 + 6)
    for to_lon, to_lat, slot, e in rim_peers:
        if e == 0:
            remote(rim_out, rim_in.at[pl.ds(3 * slot, 3)], 0, (to_lon, to_lat)).start()
        else:
            corner = 6 + 2 * slot + (0 if e == 1 else 1)
            remote(rim_out.at[pl.ds(0, 1)], rim_in.at[pl.ds(corner, 1)], 0, (to_lon, to_lat)).start()
    gain = 1.0 - inv8[0]
    carried[0] = gain
    ring_out[2] = gain
    for i in range(1, L):
        gain = gain * (1.0 - inv8[i])
        carried[i] = gain
    ring_out[0] = X[L - 1]
    ring_out[1] = gain
    ring_out[3] = X[0]
    remote(ring_out.at[pl.ds(0, 2)], ring_in.at[pl.ds(n, 2)], 1, (shifted(1), lat)).start()
    remote(ring_out.at[pl.ds(1, 3)], ring_in.at[pl.ds(0, 3)], 1, (shifted(-1), lat)).start()
    over_middle(lambda k: remote(
        ring_out.at[pl.ds(1, 1)], ring_in.at[pl.ds(k + 1, 1)], 1, (shifted(-k), lat)).start(), 2, n - 1)

    for i in range(L):
        x = X[i]
        no = jnp.where(is_north, 0.0, roll(x, 1))
        so = jnp.where(is_south, 0.0, roll(x, -1))
        u, v = winds(X, i)
        if i == 0:
            sides = X[1]
        elif i == L - 1:
            sides = X[L - 2]
        else:
            sides = X[i + 1] + X[i - 1]
        quarter = 0.25 * v
        star = x + (0.1 * (sides + no + so) - 0.4 * x) - quarter * (no - so) + (turn_u * v + turn_v * u)
        inv = inv8[i]
        fed[i] = star * inv
        edge[i] = inv * jnp.where(is_north, 0.1 - quarter, jnp.where(is_south, 0.1 + quarter, 0.0))

    wait_for(rim_in, recv_sem.at[0])

    def beside(from_north, from_south, flip):
        a = jnp.where(first, from_north * flip, roll(from_north, 1))
        b = jnp.where(last, from_south * flip, roll(from_south, -1))
        return jnp.where(even, a, b)

    center = beside(rim_in[0], rim_in[3], flips)
    packed_inv = beside(rim_in[1], rim_in[4], 1.0)
    for i in range(L):
        side_x[i] = roll(center, -2 * i)
        side_inv[i] = roll(packed_inv, -2 * i)
    outer_n = jnp.where(first, roll(rim_in[2], -1) * flips, roll(rim_in[2], 2))
    outer_s = jnp.where(last, roll(rim_in[5], 1) * flips, roll(rim_in[5], -2))
    outer = jnp.where(even, outer_n, outer_s)
    inner = rim_out[0]
    corner_w = beside(rim_in[6], rim_in[8], flips)
    corner_e = beside(rim_in[7], rim_in[9], flips)
    east = jnp.where(pair == L - 1, roll(corner_e, 2 * L - 2), roll(center, -2))
    west = jnp.where(pair == 0, roll(corner_w, 2 - 2 * L), roll(center, 2))
    no = jnp.where(even, outer, inner)
    so = jnp.where(even, inner, outer)
    rows[0] = center
    u, v = winds(rows, 0)
    star = center + (0.1 * (east + west + no + so) - 0.4 * center) - (0.25 * v) * (no - so)
    star = star + (side_turn_u * v + side_turn_v * u)
    packed_feed = star * packed_inv

    wait_for(ring_in, recv_sem.at[1])
    for i in range(L):
        rate = 1.0 - inv8[i]
        feed = fed[i] + edge[i] * side_x[i]
        if i == 0:
            feed = feed + (0.1 * inv8[i]) * ring_in[n]
        if i == L - 1:
            feed = feed + (0.1 * inv8[i]) * ring_in[2]
        side_rate = 1.0 - side_inv[i]
        side_feed = roll(packed_feed, -2 * i)
        if i == 0:
            value, side_value, side_gain = feed, side_feed, side_rate
            ends_out[0] = feed
        else:
            value = rate * value + feed
            side_value = side_rate * side_value + side_feed
            side_gain = side_gain * side_rate
        part[i] = value
        side_part[i] = side_value
        side_carried[i] = side_gain
    ends_out[1] = value
    ends_out[2] = side_value
    ends_out[3] = side_gain
    over_middle(lambda k: remote(
        ends_out.at[pl.ds(1, 3)], ends_in.at[pl.ds(3 * k - 2, 3)], 2, (shifted(-k), lat)).start(), 2, n)
    remote(ends_out, ends_in.at[pl.ds(0, 4)], 2, (shifted(-1), lat)).start()

    def gain_of(k):
        return ring_in[k + 1]

    total = gain * ring_in[0]
    total = fold(lambda k, t: t * gain_of(k), total, 2, n - 1) * ring_in[n + 1]
    ring = 1.0 / (1.0 - total)

    wait_for(ends_in, recv_sem.at[2])
    run = value * ring_in[0] + ends_in[1]
    run = fold(lambda k, r: r * gain_of(k) + ends_in[3 * k - 2], run, 2, n - 1)
    inflow = (run * ring_in[n + 1] + ends_in[3 * n - 5]) * ring

    def side_step(k, both):
        run, total = both
        return run * ends_in[3 * k] + ends_in[3 * k - 1], total * ends_in[3 * k]

    side_run, side_total = fold(side_step, (side_value, side_gain), 1, n)
    side_inflow = side_run / (1.0 - side_total)

    last_cell = value + gain * inflow
    mid_w = 0.5 * (ring_in[n] + inflow)
    mid_e = 0.5 * (ring_in[2] + (ends_in[0] + ring_in[1] * last_cell))
    for i in range(L):
        mid[i] = 0.5 * (X[i] + (part[i] + carried[i] * inflow))
    for i in range(L):
        x = mid[i]
        beyond = 0.5 * (side_x[i] + (side_part[i] + side_carried[i] * side_inflow))
        no = jnp.where(is_north, beyond, roll(x, 1))
        so = jnp.where(is_south, beyond, roll(x, -1))
        e = mid[i + 1] if i + 1 < L else mid_e
        w = mid[i - 1] if i > 0 else mid_w
        u, v = winds(mid, i)
        star = X[i] + (0.1 * (e + w + no + so) - 0.4 * x) - (0.25 * v) * (no - so) + (turn_u * v + turn_v * u)
        inv = inv8[i]
        feed = star * inv
        value = feed if i == 0 else (1.0 - inv) * value + feed
        part[i] = value
    last_out[...] = value
    over_middle(lambda k: remote(
        last_out, last_in.at[k - 1], 3, (shifted(-k), lat)).start(), 1, n)
    wait_for(last_in, recv_sem.at[3])
    run = value * ring_in[0] + last_in[0]
    run = fold(lambda k, r: r * gain_of(k) + last_in[k - 1], run, 2, n - 1)
    inflow = (run * ring_in[n + 1] + last_in[n - 2]) * ring
    for i in range(L):
        result = part[i] + carried[i] * inflow
        for l in range(levels):
            out_ref[l, i] = result[l * comps:(l + 1) * comps]
    for sem, ref in enumerate((rim_in, ring_in, ends_in, last_in)):
        wait_for(ref, send_sem.at[sem])


def local(n, m, state, courant, band_mask):
    levels, comps, L, R = state.shape
    S = levels * comps
    f32 = jnp.float32

    def cells(count):
        return pltpu.VMEM((count, S, R), f32)

    out = pl.pallas_call(
        functools.partial(kernel, n, m),
        out_shape=jax.ShapeDtypeStruct((levels, L, comps, R), f32),
        in_specs=[pl.BlockSpec(memory_space=pltpu.HBM)] * 3,
        out_specs=pl.BlockSpec(memory_space=pltpu.VMEM),
        scratch_shapes=[
            pltpu.VMEM((levels, L, comps, R), f32),
            pltpu.VMEM((L, levels, R), f32),
            pltpu.VMEM((1, R), jnp.int32),
            *[cells(L)] * 11,
            cells(1),
            cells(3),
            cells(10),
            cells(4),
            cells(n + 2),
            cells(4),
            cells(3 * n - 2),
            pltpu.VMEM((S, R), f32),
            cells(n - 1),
            pltpu.SemaphoreType.DMA((3,)),
            pltpu.SemaphoreType.DMA((4,)),
            pltpu.SemaphoreType.DMA((4,)),
        ],
        compiler_params=pltpu.CompilerParams(
            collective_id=0, has_side_effects=True, vmem_limit_bytes=64 * 2**20 - 2**17),
    )(state.transpose(0, 2, 1, 3), courant.transpose(1, 0, 2), band_mask.reshape(1, R))
    return out.transpose(0, 2, 1, 3)


def solution(mesh):
    n, m = mesh.shape["lon"], mesh.shape["lat"]
    in_specs = (P(None, None, "lon", "lat"), P(None, "lon", "lat"), P("lat"))
    out_specs = P(None, None, "lon", "lat")
    return jax.shard_map(functools.partial(local, n, m), mesh=mesh, in_specs=in_specs, out_specs=out_specs, check_vma=False)
```

```python
import functools

import jax
import jax.numpy as jnp
from jax import lax
from jax.experimental import pallas as pl
from jax.experimental.pallas import tpu as pltpu
from jax.sharding import PartitionSpec as P

MESH = pl.DeviceIdType.MESH


def kernel(n, m, x_hbm, c_hbm, mask_hbm, out_ref, x_in, c_in, mask_ref, X, inv8, carried, part, fed, edge, mid,
           side_inv, side_x, side_part, side_carried, rows,
           rim_out, rim_in, column_in, ring_out, ring_in, ends_out, ends_in, last_out, last_in,
           in_sem, send_sem, recv_sem):
    levels, L, comps, R = x_in.shape
    S = levels * comps
    lon = lax.axis_index("lon")
    lat = lax.axis_index("lat")
    first = lat == 0
    last = lat == m - 1
    north_lat = jnp.where(first, lat, lat - 1)
    south_lat = jnp.where(last, lat, lat + 1)
    north_shift = jnp.where(first, n // 2, 0)
    south_shift = jnp.where(last, n // 2, 0)
    north_slot = jnp.where(first, 0, 1)
    south_slot = jnp.where(last, 1, 0)

    def shifted(k):
        return lax.rem(lon + (k + n), n)

    rim_peers = [
        (shifted(shift + e), to_lat, slot, e)
        for e in (0, 1, -1)
        for shift, to_lat, slot in ((north_shift, north_lat, north_slot), (south_shift, south_lat, south_slot))
    ]

    def over_middle(step, low, high):
        if n <= 16:
            for k in range(low, high):
                step(k)
        else:
            lax.fori_loop(low, high, lambda k, _: (step(k), 0)[1], 0)

    barrier = pltpu.get_barrier_semaphore()
    x_copy = pltpu.make_async_copy(x_hbm, x_in, in_sem.at[0])
    c_copy = pltpu.make_async_copy(c_hbm, c_in, in_sem.at[1])
    mask_copy = pltpu.make_async_copy(mask_hbm, mask_ref, in_sem.at[2])
    x_copy.start()
    c_copy.start()
    mask_copy.start()
    for to_lon, to_lat, _, _ in rim_peers:
        pl.semaphore_signal(barrier, inc=1, device_id=(to_lon, to_lat), device_id_type=MESH)
    over_middle(lambda k: pl.semaphore_signal(
        barrier, inc=1, device_id=(shifted(k), lat), device_id_type=MESH), 1, n)

    sub = lax.broadcasted_iota(jnp.int32, (S, R), 0)
    lane = lax.broadcasted_iota(jnp.int32, (S, R), 1)
    comp = sub % comps
    lower = sub < comps
    is_north = lane == 0
    is_south = lane == R - 1
    even = lane % 2 == 0
    pair = ((lane + 1) % R) // 2
    second_pair = jnp.where(even, ((lane + 2) % R) // 2, lane // 2)

    def roll(value, shift):
        shift = shift % R
        return pltpu.roll(value, shift, 1) if shift else value

    def by_level(values):
        return jnp.where(lower, jnp.broadcast_to(values[0], (S, R)), jnp.broadcast_to(values[1], (S, R)))

    def winds(ref, i):
        u = by_level([ref[i, l * comps:l * comps + 1, :] for l in range(levels)])
        v = by_level([ref[i, l * comps + 1:l * comps + 2, :] for l in range(levels)])
        return u, v

    def turns(row_ids):
        turning = 0.5 * jnp.sin(jnp.pi / 2 - (row_ids.astype(jnp.float32) + 0.5) * (jnp.pi / (R * m)))
        return jnp.where(comp == 0, turning, 0.0), jnp.where(comp == 1, -turning, 0.0)

    turn_u, turn_v = turns(lat * R + lane)
    side_turn_u, side_turn_v = turns(jnp.where(
        even, jnp.where(first, 0, lat * R - 1), jnp.where(last, R * m - 1, lat * R + R)))
    flips = jnp.where(comp < 2, -1.0, 1.0)

    def remote(src, dst, sem, device):
        return pltpu.make_async_remote_copy(
            src_ref=src, dst_ref=dst, send_sem=send_sem.at[sem], recv_sem=recv_sem.at[sem],
            device_id=device, device_id_type=MESH)

    def wait_for(ref, sem):
        pltpu.make_async_copy(ref, ref, sem).wait()

    def fold(step, start, low, high):
        if n <= 16:
            for k in range(low, high):
                start = step(k, start)
            return start
        return lax.fori_loop(low, high, step, start)

    x_copy.wait()
    for i in range(L):
        value = jnp.concatenate([x_in[l, i] for l in range(levels)], axis=0)
        X[i] = value
        moved = roll(value, 2 * i)
        rim0 = moved if i == 0 else jnp.where(pair == i, moved, rim0)
        rim1 = moved if i == 0 else jnp.where(second_pair == i, moved, rim1)
    rim_out[0] = rim0
    rim_out[2] = rim1
    c_copy.wait()
    mask_copy.wait()
    band = mask_ref[...] == 1
    for i in range(L):
        inv = jnp.where(band, 1.0 / (1.0 + c_in[i]), 1.0)
        inv = by_level([inv[l:l + 1] for l in range(levels)])
        inv8[i] = inv
        moved = roll(inv, 2 * i)
        rim2 = moved if i == 0 else jnp.where(pair == i, moved, rim2)
    rim_out[1] = rim2

    pl.semaphore_wait(barrier, n - 1 + 6)
    for to_lon, to_lat, slot, e in rim_peers:
        if e == 1 and slot is north_slot:
            remote(X.at[pl.ds(L - 1, 1)], column_in.at[pl.ds(0, 1)], 4, (shifted(1), lat)).start()
            remote(X.at[pl.ds(0, 1)], column_in.at[pl.ds(1, 1)], 4, (shifted(-1), lat)).start()
        if e == 0:
            remote(rim_out, rim_in.at[pl.ds(3 * slot, 3)], 0, (to_lon, to_lat)).start()
        else:
            corner = 6 + 2 * slot + (0 if e == 1 else 1)
            remote(rim_out.at[pl.ds(0, 1)], rim_in.at[pl.ds(corner, 1)], 0, (to_lon, to_lat)).start()
    gain = 1.0 - inv8[0]
    carried[0] = gain
    ring_out[1] = gain
    for i in range(1, L):
        gain = gain * (1.0 - inv8[i])
        carried[i] = gain
    ring_out[0] = gain
    remote(ring_out, ring_in.at[pl.ds(0, 2)], 1, (shifted(-1), lat)).start()
    over_middle(lambda k: remote(
        ring_out.at[pl.ds(0, 1)], ring_in.at[pl.ds(k, 1)], 1, (shifted(-k), lat)).start(), 2, n)

    for i in range(L):
        x = X[i]
        no = jnp.where(is_north, 0.0, roll(x, 1))
        so = jnp.where(is_south, 0.0, roll(x, -1))
        u, v = winds(X, i)
        if i == 0:
            sides = X[1]
        elif i == L - 1:
            sides = X[L - 2]
        else:
            sides = X[i + 1] + X[i - 1]
        quarter = 0.25 * v
        star = x + (0.1 * (sides + no + so) - 0.4 * x) - quarter * (no - so) + (turn_u * v + turn_v * u)
        inv = inv8[i]
        fed[i] = star * inv
        edge[i] = inv * jnp.where(is_north, 0.1 - quarter, jnp.where(is_south, 0.1 + quarter, 0.0))

    wait_for(rim_in, recv_sem.at[0])

    def beside(from_north, from_south, flip):
        a = jnp.where(first, from_north * flip, roll(from_north, 1))
        b = jnp.where(last, from_south * flip, roll(from_south, -1))
        return jnp.where(even, a, b)

    center = beside(rim_in[0], rim_in[3], flips)
    packed_inv = beside(rim_in[1], rim_in[4], 1.0)
    for i in range(L):
        side_x[i] = roll(center, -2 * i)
        side_inv[i] = roll(packed_inv, -2 * i)
    outer_n = jnp.where(first, roll(rim_in[2], -1) * flips, roll(rim_in[2], 2))
    outer_s = jnp.where(last, roll(rim_in[5], 1) * flips, roll(rim_in[5], -2))
    outer = jnp.where(even, outer_n, outer_s)
    inner = rim_out[0]
    corner_w = beside(rim_in[6], rim_in[8], flips)
    corner_e = beside(rim_in[7], rim_in[9], flips)
    east = jnp.where(pair == L - 1, roll(corner_e, 2 * L - 2), roll(center, -2))
    west = jnp.where(pair == 0, roll(corner_w, 2 - 2 * L), roll(center, 2))
    no = jnp.where(even, outer, inner)
    so = jnp.where(even, inner, outer)
    rows[0] = center
    u, v = winds(rows, 0)
    star = center + (0.1 * (east + west + no + so) - 0.4 * center) - (0.25 * v) * (no - so)
    star = star + (side_turn_u * v + side_turn_v * u)
    packed_feed = star * packed_inv

    wait_for(column_in, recv_sem.at[4])
    for i in range(L):
        rate = 1.0 - inv8[i]
        feed = fed[i] + edge[i] * side_x[i]
        if i == 0:
            feed = feed + (0.1 * inv8[i]) * column_in[0]
        if i == L - 1:
            feed = feed + (0.1 * inv8[i]) * column_in[1]
        side_rate = 1.0 - side_inv[i]
        side_feed = roll(packed_feed, -2 * i)
        if i == 0:
            value, side_value, side_gain = feed, side_feed, side_rate
            ends_out[0] = feed
        else:
            value = rate * value + feed
            side_value = side_rate * side_value + side_feed
            side_gain = side_gain * side_rate
        part[i] = value
        side_part[i] = side_value
        side_carried[i] = side_gain
    ends_out[1] = value
    ends_out[2] = side_value
    ends_out[3] = side_gain
    over_middle(lambda k: remote(
        ends_out.at[pl.ds(1, 3)], ends_in.at[pl.ds(3 * k - 2, 3)], 2, (shifted(-k), lat)).start(), 2, n)
    remote(ends_out, ends_in.at[pl.ds(0, 4)], 2, (shifted(-1), lat)).start()

    def gain_of(k):
        return ring_in[k]

    wait_for(ring_in, recv_sem.at[1])
    total = gain * ring_in[0]
    total = fold(lambda k, t: t * gain_of(k), total, 2, n - 1) * ring_in[n - 1]
    ring = 1.0 / (1.0 - total)

    wait_for(ends_in, recv_sem.at[2])
    run = value * ring_in[0] + ends_in[1]
    run = fold(lambda k, r: r * gain_of(k) + ends_in[3 * k - 2], run, 2, n - 1)
    inflow = (run * ring_in[n - 1] + ends_in[3 * n - 5]) * ring

    def side_step(k, both):
        run, total = both
        return run * ends_in[3 * k] + ends_in[3 * k - 1], total * ends_in[3 * k]

    side_run, side_total = fold(side_step, (side_value, side_gain), 1, n)
    side_inflow = side_run / (1.0 - side_total)

    last_cell = value + gain * inflow
    mid_w = 0.5 * (column_in[0] + inflow)
    mid_e = 0.5 * (column_in[1] + (ends_in[0] + ring_in[1] * last_cell))
    for i in range(L):
        mid[i] = 0.5 * (X[i] + (part[i] + carried[i] * inflow))
    for i in range(L):
        x = mid[i]
        beyond = 0.5 * (side_x[i] + (side_part[i] + side_carried[i] * side_inflow))
        no = jnp.where(is_north, beyond, roll(x, 1))
        so = jnp.where(is_south, beyond, roll(x, -1))
        e = mid[i + 1] if i + 1 < L else mid_e
        w = mid[i - 1] if i > 0 else mid_w
        u, v = winds(mid, i)
        star = X[i] + (0.1 * (e + w + no + so) - 0.4 * x) - (0.25 * v) * (no - so) + (turn_u * v + turn_v * u)
        inv = inv8[i]
        feed = star * inv
        value = feed if i == 0 else (1.0 - inv) * value + feed
        part[i] = value
    last_out[...] = value
    over_middle(lambda k: remote(
        last_out, last_in.at[k - 1], 3, (shifted(-k), lat)).start(), 1, n)
    wait_for(last_in, recv_sem.at[3])
    run = value * ring_in[0] + last_in[0]
    run = fold(lambda k, r: r * gain_of(k) + last_in[k - 1], run, 2, n - 1)
    inflow = (run * ring_in[n - 1] + last_in[n - 2]) * ring
    for i in range(L):
        result = part[i] + carried[i] * inflow
        for l in range(levels):
            out_ref[l, i] = result[l * comps:(l + 1) * comps]
    for sem, ref in enumerate((rim_in, ring_in, ends_in, last_in, column_in)):
        wait_for(ref, send_sem.at[sem])


def local(n, m, state, courant, band_mask):
    levels, comps, L, R = state.shape
    S = levels * comps
    f32 = jnp.float32

    def cells(count):
        return pltpu.VMEM((count, S, R), f32)

    out = pl.pallas_call(
        functools.partial(kernel, n, m),
        out_shape=jax.ShapeDtypeStruct((levels, L, comps, R), f32),
        in_specs=[pl.BlockSpec(memory_space=pltpu.HBM)] * 3,
        out_specs=pl.BlockSpec(memory_space=pltpu.VMEM),
        scratch_shapes=[
            pltpu.VMEM((levels, L, comps, R), f32),
            pltpu.VMEM((L, levels, R), f32),
            pltpu.VMEM((1, R), jnp.int32),
            *[cells(L)] * 11,
            cells(1),
            cells(3),
            cells(10),
            cells(2),
            cells(2),
            cells(n),
            cells(4),
            cells(3 * n - 2),
            pltpu.VMEM((S, R), f32),
            cells(n - 1),
            pltpu.SemaphoreType.DMA((3,)),
            pltpu.SemaphoreType.DMA((5,)),
            pltpu.SemaphoreType.DMA((5,)),
        ],
        compiler_params=pltpu.CompilerParams(
            collective_id=0, has_side_effects=True, vmem_limit_bytes=16 * 2**20),
    )(*[
        pltpu.with_memory_space_constraint(value, pltpu.HBM)
        for value in (state.transpose(0, 2, 1, 3), courant.transpose(1, 0, 2), band_mask.reshape(1, R))
    ])
    return out.transpose(0, 2, 1, 3)


def solution(mesh):
    n, m = mesh.shape["lon"], mesh.shape["lat"]
    in_specs = (P(None, None, "lon", "lat"), P(None, "lon", "lat"), P("lat"))
    out_specs = P(None, None, "lon", "lat")
    return jax.shard_map(functools.partial(local, n, m), mesh=mesh, in_specs=in_specs, out_specs=out_specs, check_vma=False)
```

```python
import functools

import jax
import jax.numpy as jnp
from jax import lax
from jax.experimental import pallas as pl
from jax.experimental.pallas import tpu as pltpu
from jax.sharding import PartitionSpec as P

MESH = pl.DeviceIdType.MESH


def kernel(n, m, x_hbm, c_hbm, mask_hbm, out_ref, x_in, c_in, mask_ref, X, inv8, carried, part, fed, edge, mid,
           side_inv, side_x, side_part, side_carried, rows,
           rim_out, rim_in, column_in, ring_out, ring_in, ends_out, ends_in, last_out, last_in,
           in_sem, send_sem, recv_sem):
    levels, L, comps, R = x_in.shape
    S = levels * comps
    lon = lax.axis_index("lon")
    lat = lax.axis_index("lat")
    first = lat == 0
    last = lat == m - 1
    north_lat = jnp.where(first, lat, lat - 1)
    south_lat = jnp.where(last, lat, lat + 1)
    north_shift = jnp.where(first, n // 2, 0)
    south_shift = jnp.where(last, n // 2, 0)
    north_slot = jnp.where(first, 0, 1)
    south_slot = jnp.where(last, 1, 0)

    def shifted(k):
        return lax.rem(lon + (k + n), n)

    rim_peers = [
        (shifted(shift + e), to_lat, slot, e)
        for e in (0, 1, -1)
        for shift, to_lat, slot in ((north_shift, north_lat, north_slot), (south_shift, south_lat, south_slot))
    ]

    def over_middle(step, low, high):
        if n <= 16:
            for k in range(low, high):
                step(k)
        else:
            lax.fori_loop(low, high, lambda k, _: (step(k), 0)[1], 0)

    barrier = pltpu.get_barrier_semaphore()
    x_copy = pltpu.make_async_copy(x_hbm, x_in, in_sem.at[0])
    c_copy = pltpu.make_async_copy(c_hbm, c_in, in_sem.at[1])
    mask_copy = pltpu.make_async_copy(mask_hbm, mask_ref, in_sem.at[2])
    x_copy.start()
    for to_lon, to_lat, _, _ in rim_peers:
        pl.semaphore_signal(barrier, inc=1, device_id=(to_lon, to_lat), device_id_type=MESH)
    over_middle(lambda k: pl.semaphore_signal(
        barrier, inc=1, device_id=(shifted(k), lat), device_id_type=MESH), 1, n)

    c_copy.start()
    mask_copy.start()
    sub = lax.broadcasted_iota(jnp.int32, (S, R), 0)
    lane = lax.broadcasted_iota(jnp.int32, (S, R), 1)
    comp = sub % comps
    lower = sub < comps
    is_north = lane == 0
    is_south = lane == R - 1
    even = lane % 2 == 0
    pair = ((lane + 1) % R) // 2
    second_pair = jnp.where(even, ((lane + 2) % R) // 2, lane // 2)

    def roll(value, shift):
        shift = shift % R
        return pltpu.roll(value, shift, 1) if shift else value

    def by_level(values):
        return jnp.where(lower, jnp.broadcast_to(values[0], (S, R)), jnp.broadcast_to(values[1], (S, R)))

    def winds(ref, i):
        u = by_level([ref[i, l * comps:l * comps + 1, :] for l in range(levels)])
        v = by_level([ref[i, l * comps + 1:l * comps + 2, :] for l in range(levels)])
        return u, v

    def turns(row_ids):
        turning = 0.5 * jnp.sin(jnp.pi / 2 - (row_ids.astype(jnp.float32) + 0.5) * (jnp.pi / (R * m)))
        return jnp.where(comp == 0, turning, 0.0), jnp.where(comp == 1, -turning, 0.0)

    turn_u, turn_v = turns(lat * R + lane)
    side_turn_u, side_turn_v = turns(jnp.where(
        even, jnp.where(first, 0, lat * R - 1), jnp.where(last, R * m - 1, lat * R + R)))
    flips = jnp.where(comp < 2, -1.0, 1.0)

    def remote(src, dst, sem, device):
        return pltpu.make_async_remote_copy(
            src_ref=src, dst_ref=dst, send_sem=send_sem.at[sem], recv_sem=recv_sem.at[sem],
            device_id=device, device_id_type=MESH)

    def wait_for(ref, sem):
        pltpu.make_async_copy(ref, ref, sem).wait()

    def fold(step, start, low, high):
        if n <= 16:
            for k in range(low, high):
                start = step(k, start)
            return start
        return lax.fori_loop(low, high, step, start)

    x_copy.wait()
    for i in range(L):
        value = jnp.concatenate([x_in[l, i] for l in range(levels)], axis=0)
        X[i] = value
        moved = roll(value, 2 * i)
        rim0 = moved if i == 0 else jnp.where(pair == i, moved, rim0)
        rim1 = moved if i == 0 else jnp.where(second_pair == i, moved, rim1)
    rim_out[0] = rim0
    rim_out[2] = rim1
    c_copy.wait()
    mask_copy.wait()
    band = mask_ref[...] == 1
    for i in range(L):
        inv = jnp.where(band, 1.0 / (1.0 + c_in[i]), 1.0)
        inv = by_level([inv[l:l + 1] for l in range(levels)])
        inv8[i] = inv
        moved = roll(inv, 2 * i)
        rim2 = moved if i == 0 else jnp.where(pair == i, moved, rim2)
    rim_out[1] = rim2

    pl.semaphore_wait(barrier, n - 1 + 6)
    for to_lon, to_lat, slot, e in rim_peers:
        if e == 1 and slot is north_slot:
            remote(X.at[pl.ds(L - 1, 1)], column_in.at[pl.ds(0, 1)], 4, (shifted(1), lat)).start()
            remote(X.at[pl.ds(0, 1)], column_in.at[pl.ds(1, 1)], 4, (shifted(-1), lat)).start()
        if e == 0:
            remote(rim_out, rim_in.at[pl.ds(3 * slot, 3)], 0, (to_lon, to_lat)).start()
        else:
            corner = 6 + 2 * slot + (0 if e == 1 else 1)
            remote(rim_out.at[pl.ds(0, 1)], rim_in.at[pl.ds(corner, 1)], 0, (to_lon, to_lat)).start()
    gain = 1.0 - inv8[0]
    carried[0] = gain
    ring_out[1] = gain
    for i in range(1, L):
        gain = gain * (1.0 - inv8[i])
        carried[i] = gain
    ring_out[0] = gain
    remote(ring_out, ring_in.at[pl.ds(0, 2)], 1, (shifted(-1), lat)).start()
    over_middle(lambda k: remote(
        ring_out.at[pl.ds(0, 1)], ring_in.at[pl.ds(k, 1)], 1, (shifted(-k), lat)).start(), 2, n)

    for i in range(L):
        x = X[i]
        no = jnp.where(is_north, 0.0, roll(x, 1))
        so = jnp.where(is_south, 0.0, roll(x, -1))
        u, v = winds(X, i)
        if i == 0:
            sides = X[1]
        elif i == L - 1:
            sides = X[L - 2]
        else:
            sides = X[i + 1] + X[i - 1]
        quarter = 0.25 * v
        star = x + (0.1 * (sides + no + so) - 0.4 * x) - quarter * (no - so) + (turn_u * v + turn_v * u)
        inv = inv8[i]
        fed[i] = star * inv
        edge[i] = inv * jnp.where(is_north, 0.1 - quarter, jnp.where(is_south, 0.1 + quarter, 0.0))

    wait_for(rim_in, recv_sem.at[0])

    def beside(from_north, from_south, flip):
        a = jnp.where(first, from_north * flip, roll(from_north, 1))
        b = jnp.where(last, from_south * flip, roll(from_south, -1))
        return jnp.where(even, a, b)

    center = beside(rim_in[0], rim_in[3], flips)
    packed_inv = beside(rim_in[1], rim_in[4], 1.0)
    for i in range(L):
        side_x[i] = roll(center, -2 * i)
        side_inv[i] = roll(packed_inv, -2 * i)
    outer_n = jnp.where(first, roll(rim_in[2], -1) * flips, roll(rim_in[2], 2))
    outer_s = jnp.where(last, roll(rim_in[5], 1) * flips, roll(rim_in[5], -2))
    outer = jnp.where(even, outer_n, outer_s)
    inner = rim_out[0]
    corner_w = beside(rim_in[6], rim_in[8], flips)
    corner_e = beside(rim_in[7], rim_in[9], flips)
    east = jnp.where(pair == L - 1, roll(corner_e, 2 * L - 2), roll(center, -2))
    west = jnp.where(pair == 0, roll(corner_w, 2 - 2 * L), roll(center, 2))
    no = jnp.where(even, outer, inner)
    so = jnp.where(even, inner, outer)
    rows[0] = center
    u, v = winds(rows, 0)
    star = center + (0.1 * (east + west + no + so) - 0.4 * center) - (0.25 * v) * (no - so)
    star = star + (side_turn_u * v + side_turn_v * u)
    packed_feed = star * packed_inv

    wait_for(column_in, recv_sem.at[4])
    for i in range(L):
        rate = 1.0 - inv8[i]
        feed = fed[i] + edge[i] * side_x[i]
        if i == 0:
            feed = feed + (0.1 * inv8[i]) * column_in[0]
        if i == L - 1:
            feed = feed + (0.1 * inv8[i]) * column_in[1]
        side_rate = 1.0 - side_inv[i]
        side_feed = roll(packed_feed, -2 * i)
        if i == 0:
            value, side_value, side_gain = feed, side_feed, side_rate
            ends_out[0] = feed
        else:
            value = rate * value + feed
            side_value = side_rate * side_value + side_feed
            side_gain = side_gain * side_rate
        part[i] = value
        side_part[i] = side_value
        side_carried[i] = side_gain
    ends_out[1] = value
    ends_out[2] = side_value
    ends_out[3] = side_gain
    over_middle(lambda k: remote(
        ends_out.at[pl.ds(1, 3)], ends_in.at[pl.ds(3 * k - 2, 3)], 2, (shifted(-k), lat)).start(), 2, n)
    remote(ends_out, ends_in.at[pl.ds(0, 4)], 2, (shifted(-1), lat)).start()

    def gain_of(k):
        return ring_in[k]

    wait_for(ring_in, recv_sem.at[1])
    total = gain * ring_in[0]
    total = fold(lambda k, t: t * gain_of(k), total, 2, n - 1) * ring_in[n - 1]
    ring = 1.0 / (1.0 - total)

    wait_for(ends_in, recv_sem.at[2])
    run = value * ring_in[0] + ends_in[1]
    run = fold(lambda k, r: r * gain_of(k) + ends_in[3 * k - 2], run, 2, n - 1)
    inflow = (run * ring_in[n - 1] + ends_in[3 * n - 5]) * ring

    def side_step(k, both):
        run, total = both
        return run * ends_in[3 * k] + ends_in[3 * k - 1], total * ends_in[3 * k]

    side_run, side_total = fold(side_step, (side_value, side_gain), 1, n)
    side_inflow = side_run / (1.0 - side_total)

    last_cell = value + gain * inflow
    mid_w = 0.5 * (column_in[0] + inflow)
    mid_e = 0.5 * (column_in[1] + (ends_in[0] + ring_in[1] * last_cell))
    for i in range(L):
        mid[i] = 0.5 * (X[i] + (part[i] + carried[i] * inflow))
    for i in range(L):
        x = mid[i]
        beyond = 0.5 * (side_x[i] + (side_part[i] + side_carried[i] * side_inflow))
        no = jnp.where(is_north, beyond, roll(x, 1))
        so = jnp.where(is_south, beyond, roll(x, -1))
        e = mid[i + 1] if i + 1 < L else mid_e
        w = mid[i - 1] if i > 0 else mid_w
        u, v = winds(mid, i)
        star = X[i] + (0.1 * (e + w + no + so) - 0.4 * x) - (0.25 * v) * (no - so) + (turn_u * v + turn_v * u)
        inv = inv8[i]
        feed = star * inv
        value = feed if i == 0 else (1.0 - inv) * value + feed
        part[i] = value
    last_out[...] = value
    over_middle(lambda k: remote(
        last_out, last_in.at[k - 1], 3, (shifted(-k), lat)).start(), 2, n)
    remote(last_out, last_in.at[0], 3, (shifted(-1), lat)).start()
    wait_for(last_in, recv_sem.at[3])
    run = value * ring_in[0] + last_in[0]
    run = fold(lambda k, r: r * gain_of(k) + last_in[k - 1], run, 2, n - 1)
    inflow = (run * ring_in[n - 1] + last_in[n - 2]) * ring
    for i in range(L):
        result = part[i] + carried[i] * inflow
        for l in range(levels):
            out_ref[l, i] = result[l * comps:(l + 1) * comps]
    for sem, ref in enumerate((rim_in, ring_in, ends_in, last_in, column_in)):
        wait_for(ref, send_sem.at[sem])


def local(n, m, state, courant, band_mask):
    levels, comps, L, R = state.shape
    S = levels * comps
    f32 = jnp.float32

    def cells(count):
        return pltpu.VMEM((count, S, R), f32)

    out = pl.pallas_call(
        functools.partial(kernel, n, m),
        out_shape=jax.ShapeDtypeStruct((levels, L, comps, R), f32),
        in_specs=[pl.BlockSpec(memory_space=pltpu.HBM)] * 3,
        out_specs=pl.BlockSpec(memory_space=pltpu.VMEM),
        scratch_shapes=[
            pltpu.VMEM((levels, L, comps, R), f32),
            pltpu.VMEM((L, levels, R), f32),
            pltpu.VMEM((1, R), jnp.int32),
            *[cells(L)] * 11,
            cells(1),
            cells(3),
            cells(10),
            cells(2),
            cells(2),
            cells(n),
            cells(4),
            cells(3 * n - 2),
            pltpu.VMEM((S, R), f32),
            cells(n - 1),
            pltpu.SemaphoreType.DMA((3,)),
            pltpu.SemaphoreType.DMA((5,)),
            pltpu.SemaphoreType.DMA((5,)),
        ],
        compiler_params=pltpu.CompilerParams(
            collective_id=0, has_side_effects=True, vmem_limit_bytes=16 * 2**20),
    )(*[
        pltpu.with_memory_space_constraint(value, pltpu.HBM)
        for value in (state.transpose(0, 2, 1, 3), courant.transpose(1, 0, 2), band_mask.reshape(1, R))
    ])
    return out.transpose(0, 2, 1, 3)


def solution(mesh):
    n, m = mesh.shape["lon"], mesh.shape["lat"]
    in_specs = (P(None, None, "lon", "lat"), P(None, "lon", "lat"), P("lat"))
    out_specs = P(None, None, "lon", "lat")
    return jax.shard_map(functools.partial(local, n, m), mesh=mesh, in_specs=in_specs, out_specs=out_specs, check_vma=False)
```
